32 devices in a mesh: rows: 8 (over z, core), cols: 4 (over y, x).
Axes of the slice: x: 2, y: 2, z: 4, core: 2. Of those that a mesh axis runs over, the one named last changes fastest.
Arguments:
- gradient: float32 [6144, 28672], P('rows', 'cols'), may hold values from -6 to 6
- basis: float32 [8, 28672, 128], P('rows', 'cols'), may hold values from -0.03125 to 0.03125
- panel_index: int32 [4], replicated, may hold values from 0 to 7, as said below
- input_eigen: float32 [8192], replicated, may hold values from 0.1 to 3
- output_eigen: float32 [28672], replicated, may hold values from 0.1 to 3
- input_pick: int32 [4, 128], replicated, may hold values from 0 to 8191
- output_pick: int32 [4, 128], replicated, may hold values from 0 to 28671
Outputs:
- preconditioned: float32 [6144, 28672], P('rows', 'cols')
The draws below stay inside these ranges and needn't reach their ends.
Inputs may be any that keep to these rules, and one draw needn't show every extreme that they name: `panel_index`: the 4 entries are distinct.
All inputs are finite; a program needn't handle non-finite values.
Results may differ from the reference program's by a relative error of at most 0.0001.
Values sent between devices are 32-bit elements; how exact they have to be, the bound alone decides.
A program may use at most 192 MiB of HBM per device.

```python
import math
import jax
import jax.numpy as jnp
from jax import lax

D = 8192
M = 28672
PANEL = 128
NSEL = 4
PSTOCK = 8
R = 6144


def draw_panel_index(key, part):
    middle = jax.random.permutation(jax.random.fold_in(key, 11), PSTOCK - 2)[:NSEL - 2] + 1
    ends = jnp.array([0, PSTOCK - 1], jnp.int32)
    picked = jnp.concatenate([ends, middle.astype(jnp.int32)])
    order = jax.random.permutation(jax.random.fold_in(key, 13), NSEL)
    return picked[order].astype(jnp.int32)


def place_ends(values, own_key, smallest, high):
    dims = values.shape
    place = [jax.random.randint(jax.random.fold_in(own_key, axis), (), 0, dims[axis]) for axis in range(len(dims))]
    values = values.at[tuple(place)].set(smallest)
    longest = dims.index(max(dims))
    place[longest] = (place[longest] + 1) % dims[longest]
    return values.at[tuple(place)].set(high)


def block_scale(own_key, extent, split, least, high):
    gain, own = 1.0, jax.random.fold_in(own_key, 6)
    for position, shards_of in split:
        heights = jnp.exp(jax.random.uniform(jax.random.fold_in(own, position), (shards_of,), jnp.float32, least / len(split), high / len(split)))
        gain = gain * jnp.repeat(heights, extent[position] // shards_of).reshape([-1 if axis == position else 1 for axis in range(len(extent))])
    return gain


def noise(own_key, dims, deviation, most, split=(), held_as=jnp.bfloat16):
    level = block_scale(own_key, dims, split, -0.22, 0.18) if split else 1.0
    values = jax.random.normal(own_key, dims, jnp.float32) * deviation * level
    return jnp.minimum(jnp.maximum(values, -most), most).astype(held_as)


def setup_inputs(seed: int = 0) -> dict:
    seeds = jax.random.split(jax.random.key(seed), 8)
    return {
        "gradient": noise(seeds[0], (R, M), 1.0, 6.0, ((0, 8), (1, 4)), jnp.float32),
        "basis": noise(seeds[1], (PSTOCK, M, PANEL), M ** -0.5, 0.03125, ((0, 8), (1, 4)), jnp.float32),
        "panel_index": draw_panel_index(jax.random.fold_in(seeds[7], 71), 0),
        "input_eigen": jnp.clip(jnp.exp(jax.random.uniform(seeds[3], (D,), jnp.float32, math.log(0.1), math.log(3.0))), 0.1, 3.0),
        "output_eigen": jnp.clip(jnp.exp(jax.random.uniform(seeds[4], (M,), jnp.float32, math.log(0.1), math.log(3.0))), 0.1, 3.0),
        "input_pick": place_ends(jax.random.randint(seeds[5], (NSEL, PANEL), 0, D), jax.random.fold_in(seeds[5], 1), 0, D - 1).astype(jnp.int32),
        "output_pick": place_ends(jax.random.randint(seeds[6], (NSEL, PANEL), 0, M), jax.random.fold_in(seeds[6], 1), 0, M - 1).astype(jnp.int32),
    }


def reference(gradient, basis, panel_index, input_eigen, output_eigen, input_pick, output_pick):
    result = jnp.zeros(gradient.shape, jnp.float32)
    for number in range(NSEL):
        chosen = basis[panel_index[number]]
        projected = jnp.dot(gradient, chosen, precision=lax.Precision.HIGHEST, preferred_element_type=jnp.float32)
        damped = input_eigen[input_pick[number]] * output_eigen[output_pick[number]] + 0.05
        scaled = projected / damped[None, :]
        result = result + jnp.dot(scaled, chosen.T, precision=lax.Precision.HIGHEST, preferred_element_type=jnp.float32)
    return result
```

```python
import functools

import jax
import jax.numpy as jnp
from jax import lax
from jax.sharding import PartitionSpec as P

NSEL = 4
LAG = 2
CHUNKS = 8
PIECES = 4


def matmul(a, b):
    return lax.dot_general(
        a, b, (((1,), (0,)), ((), ())), precision=lax.Precision.HIGH, preferred_element_type=jnp.float32
    )


def matmul_t(a, b):
    return lax.dot_general(
        a, b, (((1,), (1,)), ((), ())), precision=lax.Precision.HIGH, preferred_element_type=jnp.float32
    )


def exchange_sum(value, size):
    if size & (size - 1):
        return lax.psum(value, "cols")
    bits = [1 << b for b in range(size.bit_length() - 1)]
    rows = value.shape[0] // 2
    parts = []
    for part, order in ((value[:rows], bits), (value[rows:], bits[::-1])):
        for bit in order:
            part = part + lax.ppermute(part, "cols", [(i, i ^ bit) for i in range(size)])
        parts.append(part)
    return jnp.concatenate(parts, axis=0)


def general(nrows, ncols, gradient, basis, panel_index, damped):
    everything = lax.all_gather(basis, "rows", axis=0, tiled=True)
    result = jnp.zeros(gradient.shape, jnp.float32)
    for number in range(NSEL):
        chosen = lax.dynamic_index_in_dim(everything, panel_index[number], 0, keepdims=False)
        projected = lax.psum(matmul(gradient, chosen), "cols")
        result = result + matmul_t(projected / damped[number][None, :], chosen)
    return result


def streamed(nrows, ncols, gradient, basis, panel_index, damped):
    chips = nrows // 2
    me = lax.axis_index("rows")
    chip, core = me // 2, me % 2
    own = basis[0]
    depth, width = own.shape
    half = depth // 2
    size = half // CHUNKS
    swap = [(i, i ^ 1) for i in range(nrows)]
    first = core == 0

    sent = lax.dynamic_slice_in_dim(own, (1 - core) * half, half, 0)
    kept = lax.dynamic_slice_in_dim(own, core * half, half, 0)
    got = lax.ppermute(sent, "rows", swap)
    own0, own1 = jnp.where(first, kept, got), jnp.where(first, got, kept)

    below = jnp.sum(panel_index < 2 * chip)
    above = jnp.sum(panel_index > 2 * chip + 1)
    has0 = jnp.any(panel_index == 2 * chip)
    has1 = jnp.any(panel_index == 2 * chip + 1)
    up0 = jnp.where(has0, below, -1)
    up1 = jnp.where(has1, below + has0, -1)
    down1 = jnp.where(has1, above, -1)
    down0 = jnp.where(has0, above + has1, -1)

    total = (NSEL - 1) * CHUNKS
    rounds = total + LAG * (chips - 2)

    def send_of(t, place, slot0, slot1, held):
        q = jnp.clip(t - LAG * place, 0, total - 1)
        slot, c = q // CHUNKS, q % CHUNKS
        mine0 = lax.dynamic_slice_in_dim(own0, c * size, size, 0)
        mine1 = lax.dynamic_slice_in_dim(own1, c * size, size, 0)
        other = mine0 if held is None else held
        return jnp.where(slot == slot0, mine0, jnp.where(slot == slot1, mine1, other))

    upward = [(i, i + 2) for i in range(nrows - 2)]
    downward = [(i + 2, i) for i in range(nrows - 2)]
    ups, downs = [], []
    for t in range(rounds):
        before = t - LAG
        ups.append(
            lax.ppermute(
                send_of(t, chip, up0, up1, ups[before] if before >= 0 else None), "rows", upward
            )
        )
        downs.append(
            lax.ppermute(
                send_of(t, chips - 1 - chip, down0, down1, downs[before] if before >= 0 else None),
                "rows",
                downward,
            )
        )

    def arrived(stream, place, slot, start, count):
        begin = slot * CHUNKS + start
        window = stream[begin:begin + count + LAG * (chips - 2)]
        shift = jnp.clip(LAG * (place - 1), 0, LAG * (chips - 2))
        return lax.dynamic_slice_in_dim(jnp.concatenate(window, axis=0), shift * size, count * size, 0)

    def pick(rank, start, count):
        rows = slice(start * size, (start + count) * size)
        back = NSEL - 1 - rank
        if rank == 0:
            far = arrived(ups, chip, 0, start, count)
        elif rank == NSEL - 1:
            far = arrived(downs, chips - 1 - chip, 0, start, count)
        else:
            far = jnp.where(
                below > rank,
                arrived(ups, chip, rank, start, count),
                arrived(downs, chips - 1 - chip, back, start, count),
            )
        return jnp.where(up0 == rank, own0[rows], jnp.where(up1 == rank, own1[rows], far))

    order = jnp.argsort(panel_index)
    damped = damped[order]

    def project(ranks, pieces):
        count = CHUNKS // pieces
        step = count * size
        partial, lows, highs = None, [], []
        for piece in range(pieces):
            mine = jnp.concatenate([pick(rank, piece * count, count) for rank in ranks], axis=1)
            other = lax.ppermute(mine, "rows", swap)
            low, high = jnp.where(first, mine, other), jnp.where(first, other, mine)
            at = piece * step
            term = matmul(gradient[:, at:at + step], low) + matmul(
                gradient[:, half + at:half + at + step], high
            )
            partial = term if partial is None else partial + term
            lows.append(low)
            highs.append(high)
        scale = jnp.concatenate([damped[rank] for rank in ranks])
        projected = exchange_sum(partial, ncols)
        return projected / scale[None, :], jnp.concatenate(lows + highs, axis=0)

    scaled_a, chosen_a = project((0, 3), 2)
    result = matmul_t(scaled_a, chosen_a)
    scaled_b, chosen_b = project((1, 2), PIECES)
    return result + matmul_t(scaled_b, chosen_b)


def shards(
    nrows, ncols, gradient, basis, panel_index, input_eigen, output_eigen, input_pick, output_pick
):
    damped = input_eigen[input_pick] * output_eigen[output_pick] + 0.05
    operands = (gradient, basis, panel_index, damped)
    if basis.shape[0] != 1 or nrows % 2 or nrows < 4 or basis.shape[1] % (16 * CHUNKS):
        return general(nrows, ncols, *operands)
    ends = jnp.any(panel_index < 2) & jnp.any(panel_index >= nrows - 2)
    return lax.cond(
        ends,
        functools.partial(streamed, nrows, ncols),
        functools.partial(general, nrows, ncols),
        *operands,
    )


def solution(mesh):
    in_specs = (P("rows", "cols"), P("rows", "cols", None), P(), P(), P(), P(), P())
    body = functools.partial(shards, mesh.shape["rows"], mesh.shape["cols"])
    return jax.shard_map(
        body, mesh=mesh, in_specs=in_specs, out_specs=P("rows", "cols"), check_vma=False
    )
```

```python
import functools

import jax
import jax.numpy as jnp
from jax import lax
from jax.experimental import pallas as pl
from jax.experimental.pallas import tpu as pltpu
from jax.sharding import PartitionSpec as P

NSEL = 4
LAG = 2
CHUNKS = 14
MESH = pl.DeviceIdType.MESH


def matmul(a, b):
    return lax.dot_general(
        a, b, (((1,), (0,)), ((), ())), precision=lax.Precision.HIGH, preferred_element_type=jnp.float32
    )


def matmul_t(a, b):
    return lax.dot_general(
        a, b, (((1,), (1,)), ((), ())), precision=lax.Precision.HIGH, preferred_element_type=jnp.float32
    )


def exchange_sum(value, size):
    if size & (size - 1):
        return lax.psum(value, "cols")
    bits = [1 << b for b in range(size.bit_length() - 1)]
    rows = value.shape[0] // 2
    parts = []
    for part, order in ((value[:rows], bits), (value[rows:], bits[::-1])):
        for bit in order:
            part = part + lax.ppermute(part, "cols", [(i, i ^ bit) for i in range(size)])
        parts.append(part)
    return jnp.concatenate(parts, axis=0)


def general(nrows, ncols, gradient, basis, panel_index, damped):
    everything = lax.all_gather(basis, "rows", axis=0, tiled=True)
    result = jnp.zeros(gradient.shape, jnp.float32)
    for number in range(NSEL):
        chosen = lax.dynamic_index_in_dim(everything, panel_index[number], 0, keepdims=False)
        projected = lax.psum(matmul(gradient, chosen), "cols")
        result = result + matmul_t(projected / damped[number][None, :], chosen)
    return result


def split(value):
    high = value.astype(jnp.bfloat16)
    return high, (value - high.astype(jnp.float32)).astype(jnp.bfloat16)


def three_products(a, b, contract):
    (ah, al), (bh, bl) = a, b
    dims = (((1,), (contract,)), ((), ()))
    dot = functools.partial(lax.dot_general, dimension_numbers=dims, preferred_element_type=jnp.float32)
    return dot(ah, bh) + dot(ah, bl) + dot(al, bh)


def stream_kernel(chips, half, size, slots_ref, own_hbm, pool, own, got, up_in, down_in, up_out, down_out,
                  own_sem, keep_sem, swap_send, swap_recv, give_send, give_recv,
                  up_send, up_recv, down_send, down_recv,
                  up_give_send, up_give_recv, down_give_send, down_give_recv, up_keep, down_keep):
    me = lax.axis_index("rows")
    col = lax.axis_index("cols")
    chip, core = me // 2, me % 2
    partner = (me + 1 - 2 * core, col)
    chunks = half // size
    total = (NSEL - 1) * chunks

    load = pltpu.make_async_copy(own_hbm, own, own_sem.at[0])
    load.start()
    barrier = pltpu.get_barrier_semaphore()
    pl.semaphore_signal(barrier, inc=1, device_id=partner, device_id_type=MESH)

    @pl.when(chip > 0)
    def _():
        pl.semaphore_signal(barrier, inc=1, device_id=(me - 2, col), device_id_type=MESH)

    @pl.when(chip < chips - 1)
    def _():
        pl.semaphore_signal(barrier, inc=1, device_id=(me + 2, col), device_id_type=MESH)

    inner = (chip > 0).astype(jnp.int32) + (chip < chips - 1).astype(jnp.int32)
    pl.semaphore_wait(barrier, 1 + inner)
    load.wait()

    def remote(src, dst, send, recv, device):
        return pltpu.make_async_remote_copy(
            src_ref=src, dst_ref=dst, send_sem=send, recv_sem=recv, device_id=device, device_id_type=MESH
        )

    def swap(c):
        return remote(own.at[1 - core, pl.ds(c * size, size)], got.at[pl.ds(c * size, size)],
                      swap_send.at[c], swap_recv.at[c], partner)

    def at(ref, q):
        return ref.at[pl.ds(q * size, size)]

    def landed(base, q):
        return pool.at[base + q // chunks, core, pl.ds((q % chunks) * size, size)]

    give = remote(own, pool.at[core],
                  give_send.at[0], give_recv.at[0], partner)
    keep = pltpu.make_async_copy(own, pool.at[core], keep_sem.at[0])

    @pl.loop(0, chunks)
    def _(c):
        swap(c).start()

    def turn(t, place, inbox, outbox, send, recv, gsend, grecv, ksem, base, slot0, slot1, to):
        q = t - LAG * place

        @pl.when((q >= 0) & (q < total))
        def _():
            @pl.when(place > 0)
            def _():
                remote(at(inbox, q), at(inbox, q), send.at[q], recv.at[q], partner).wait_recv()
                remote(at(inbox, q), landed(base, q), gsend.at[q], grecv.at[q], partner).start()
                pltpu.make_async_copy(at(inbox, q), landed(base, q), ksem.at[q]).start()

            @pl.when(place < chips - 1)
            def _():
                slot, c = q // chunks, q % chunks
                kept = own[core, pl.ds(c * size, size), :]
                other = got[pl.ds(c * size, size), :]
                mine0 = jnp.where(core == 0, kept, other)
                mine1 = jnp.where(core == 0, other, kept)
                outbox[pl.ds(q * size, size), :] = jnp.where(
                    slot == slot0, mine0, jnp.where(slot == slot1, mine1, inbox[pl.ds(q * size, size), :])
                )
                remote(at(outbox, q), at(inbox, q), send.at[q], recv.at[q], to).start()

    up = (up_in, up_out, up_send, up_recv, up_give_send, up_give_recv, up_keep, 2)
    down = (down_in, down_out, down_send, down_recv, down_give_send, down_give_recv, down_keep, 1 + NSEL)

    @pl.loop(0, total + LAG * (chips - 1))
    def _(t):
        @pl.when(t < chunks)
        def _():
            swap(t).wait()

        turn(t, chip, *up, slots_ref[0], slots_ref[1], (me + 2, col))
        turn(t, chips - 1 - chip, *down, slots_ref[2], slots_ref[3], (me - 2, col))

        @pl.when(t == total - 1)
        def _():
            give.start()
            keep.start()

    def drain(q, place, inbox, outbox, send, recv, gsend, grecv, ksem, base):
        @pl.when(place < chips - 1)
        def _():
            remote(at(outbox, q), at(inbox, q), send.at[q], recv.at[q], partner).wait_send()

        @pl.when(place > 0)
        def _():
            remote(at(inbox, q), landed(base, q), gsend.at[q], grecv.at[q], partner).wait()
            pltpu.make_async_copy(at(inbox, q), landed(base, q), ksem.at[q]).wait()

    @pl.loop(0, total)
    def _(q):
        drain(q, chip, *up)
        drain(q, chips - 1 - chip, *down)

    give.wait()
    keep.wait()


def project_kernel(sel_ref, g_ref, v0, v1, v2, v3, out_ref):
    @pl.when(pl.program_id(0) == 0)
    def _():
        out_ref[...] = jnp.zeros_like(out_ref)

    panels = jnp.concatenate([v[0] for v in (v0, v1, v2, v3)], axis=1)
    out_ref[...] += three_products(split(g_ref[...]), split(panels), 0)


def apply_kernel(sel_ref, s_ref, v0, v1, v2, v3, out_ref):
    panels = jnp.concatenate([v[0] for v in (v0, v1, v2, v3)], axis=1)
    out_ref[...] = three_products(split(s_ref[...]), split(panels), 1)


def streamed(nrows, ncols, gradient, basis, panel_index, damped):
    chips = nrows // 2
    chip = lax.axis_index("rows") // 2
    own = basis[0]
    depth, width = own.shape
    half = depth // 2
    size = half // CHUNKS
    rows = gradient.shape[0]

    below = jnp.sum(panel_index < 2 * chip)
    above = jnp.sum(panel_index > 2 * chip + 1)
    has0 = jnp.any(panel_index == 2 * chip)
    has1 = jnp.any(panel_index == 2 * chip + 1)
    up0 = jnp.where(has0, below, -1)
    up1 = jnp.where(has1, below + has0, -1)
    down1 = jnp.where(has1, above, -1)
    down0 = jnp.where(has0, above + has1, -1)
    slots = jnp.stack([up0, up1, down0, down1]).astype(jnp.int32)

    total = (NSEL - 1) * CHUNKS
    line = pltpu.VMEM((total * size, width), jnp.float32)
    dma = pltpu.SemaphoreType.DMA
    pool = pl.pallas_call(
        functools.partial(stream_kernel, chips, half, size),
        out_shape=jax.ShapeDtypeStruct((2 * NSEL, 2, half, width), jnp.float32),
        in_specs=[pl.BlockSpec(memory_space=pltpu.SMEM), pl.BlockSpec(memory_space=pl.ANY)],
        out_specs=pl.BlockSpec(memory_space=pl.ANY),
        scratch_shapes=[pltpu.VMEM((2, half, width), jnp.float32), pltpu.VMEM((half, width), jnp.float32)]
        + [line] * 4
        + [dma((1,))] * 2 + [dma((CHUNKS,))] * 2 + [dma((1,))] * 2 + [dma((total,))] * 10,
        compiler_params=pltpu.CompilerParams(
            collective_id=0, has_side_effects=True, vmem_limit_bytes=48 * 2**20
        ),
    )(slots, own.reshape(2, half, width))
    pool = pool.reshape(2 * NSEL, depth, width)

    ranks = jnp.arange(NSEL)
    far = jnp.where(below > ranks, 2 + ranks, 2 * NSEL - ranks)
    place = jnp.where(ranks == up0, 0, jnp.where(ranks == up1, 1, jnp.clip(far, 0, 2 * NSEL - 1)))
    place = place.astype(jnp.int32)
    damped = damped[jnp.argsort(panel_index)].reshape(1, NSEL * width)

    tile = 512 if depth % 512 == 0 else 128
    panel_specs = [
        pl.BlockSpec((1, tile, width), functools.partial(lambda r, k, sel: (sel[r], k, 0), r))
        for r in range(NSEL)
    ]
    side = pl.BlockSpec((rows, tile), lambda k, sel: (0, k))
    wide = pl.BlockSpec((rows, NSEL * width), lambda k, sel: (0, 0))
    limits = pltpu.CompilerParams(vmem_limit_bytes=48 * 2**20)
    partial = pl.pallas_call(
        project_kernel,
        out_shape=jax.ShapeDtypeStruct((rows, NSEL * width), jnp.float32),
        grid_spec=pltpu.PrefetchScalarGridSpec(
            num_scalar_prefetch=1, grid=(depth // tile,), in_specs=[side] + panel_specs, out_specs=wide
        ),
        compiler_params=limits,
    )(place, gradient, pool, pool, pool, pool)
    scaled = exchange_sum(partial, ncols) / damped
    return pl.pallas_call(
        apply_kernel,
        out_shape=jax.ShapeDtypeStruct(gradient.shape, jnp.float32),
        grid_spec=pltpu.PrefetchScalarGridSpec(
            num_scalar_prefetch=1, grid=(depth // tile,), in_specs=[wide] + panel_specs, out_specs=side
        ),
        compiler_params=limits,
    )(place, scaled, pool, pool, pool, pool)


def shards(
    nrows, ncols, gradient, basis, panel_index, input_eigen, output_eigen, input_pick, output_pick
):
    damped = input_eigen[input_pick] * output_eigen[output_pick] + 0.05
    operands = (gradient, basis, panel_index, damped)
    if basis.shape[0] != 1 or nrows % 2 or nrows < 4 or basis.shape[1] % (16 * CHUNKS):
        return general(nrows, ncols, *operands)
    ends = jnp.any(panel_index < 2) & jnp.any(panel_index >= nrows - 2)
    return lax.cond(
        ends,
        functools.partial(streamed, nrows, ncols),
        functools.partial(general, nrows, ncols),
        *operands,
    )


def solution(mesh):
    in_specs = (P("rows", "cols"), P("rows", "cols", None), P(), P(), P(), P(), P())
    body = functools.partial(shards, mesh.shape["rows"], mesh.shape["cols"])
    return jax.shard_map(
        body, mesh=mesh, in_specs=in_specs, out_specs=P("rows", "cols"), check_vma=False
    )
```
